512 devices in a mesh: section: 4 (over y_lo, core), tensor: 8 (over z), ctx: 16 (over x, y_hi).
Axes of the slice: x: 4, y: 8 (y_hi: 4, y_lo: 2; y = y_hi * 2 + y_lo), z: 8, core: 2. Of those that a mesh axis runs over, the one named last changes fastest.
Arguments:
- gate_in: bfloat16 [4, 16384, 2048], P('section', 'ctx', 'tensor'), may hold values from -6 to 6
- value_in: bfloat16 [4, 16384, 2048], P('section', 'ctx', 'tensor'), may hold values from -6 to 6
- gate_out: bfloat16 [4, 16384, 2048], P('section', 'ctx', 'tensor'), may hold values from -6 to 6
- filter_spectrum: bfloat16 [4, 256, 2, 128, 2048], P('section', 'ctx', None, None, 'tensor'), may hold values from -16 to 16
- skip: bfloat16 [4, 2048], P('section', 'tensor'), may hold values from -4 to 4
- out_weight: bfloat16 [4, 2048, 4096], P('section', 'ctx', 'tensor'), may hold values from -0.125 to 0.125
Outputs:
- mixed: bfloat16 [4, 16384, 4096], P('section', 'ctx', 'tensor')
The draws below stay inside these ranges and needn't reach their ends.
All inputs are finite; a program needn't handle non-finite values.
Results may differ from the reference program's by a relative error of at most 0.015.
Values may be sent and summed in bfloat16 or wider, within the bound.
A program may use at most 64 MiB of HBM per device.

```python
import math
import jax
import jax.numpy as jnp
from jax import lax

D = 4096
CH = 2048
COLS = 128
TOKENS = 16384
ROWS = 256
SECTIONS = 4


def pole_term(res_real, res_imag, rho, decay_all, freq, index, total):
    turns = (freq - index) % total
    phase = turns.astype(jnp.float32) * (2.0 * math.pi / total)
    parity = 1.0 - 2.0 * ((freq + index) % 2).astype(jnp.float32)
    factor = 1.0 - decay_all * parity
    num_real = res_real * factor
    num_imag = res_imag * factor
    den_real = 1.0 - rho * jnp.cos(phase)
    den_imag = -rho * jnp.sin(phase)
    norm_sq = den_real * den_real + den_imag * den_imag
    out_real = (num_real * den_real + num_imag * den_imag) / norm_sq
    out_imag = (num_imag * den_real - num_real * den_imag) / norm_sq
    return (out_real, out_imag)


def draw_filter_spectrum(key, part):
    key = jax.random.fold_in(key, 11)
    keys = jax.random.split(key, 6)
    mode_count = 2
    total = 2 * TOKENS
    clip_level = float(max(4, TOKENS // 1024))
    shape = (SECTIONS, 1, 1, CH, mode_count)
    lo_len = math.log(30.0)
    memory = jnp.exp(jax.random.uniform(keys[0], shape, jnp.float32, lo_len, math.log(16.0 * TOKENS)))
    rho = jnp.exp(-1.0 / memory)
    decay_all = jnp.exp(-TOKENS / memory)
    freq = jax.random.randint(keys[1], shape, 0, total)
    amp = jnp.exp(jax.random.uniform(keys[2], shape, jnp.float32, math.log(0.5), math.log(1.5)))
    amp = amp * jnp.sqrt(1.0 - rho * rho)
    angle = jax.random.uniform(keys[3], shape, jnp.float32, 0.0, 2.0 * math.pi)
    res_real = amp * jnp.cos(angle)
    res_imag = amp * jnp.sin(angle)
    row_idx = jnp.arange(ROWS, dtype=jnp.int32)[:, None]
    col_idx = jnp.arange(COLS, dtype=jnp.int32)[None, :]
    index = (row_idx + ROWS * col_idx)[None, :, :, None]
    sum_real = jax.random.normal(keys[4], (SECTIONS, ROWS, COLS, CH), jnp.float32)
    sum_imag = jax.random.normal(keys[5], (SECTIONS, ROWS, COLS, CH), jnp.float32)
    for which in range(mode_count):
        first = pole_term(res_real[..., which], res_imag[..., which], rho[..., which], decay_all[..., which], freq[..., which], index, total)
        second = pole_term(res_real[..., which], -res_imag[..., which], rho[..., which], decay_all[..., which], (total - freq[..., which]) % total, index, total)
        sum_real = sum_real + 0.5 * (first[0] + second[0])
        sum_imag = sum_imag + 0.5 * (first[1] + second[1])
    sum_real = jnp.clip(sum_real, -clip_level, clip_level)
    sum_imag = jnp.clip(sum_imag, -clip_level, clip_level)
    return jnp.stack([sum_real, sum_imag], axis=2).astype(jnp.bfloat16)


def level_of(stream_key, extent, shards, low, high):
    gain = 1.0
    for axis_at, blocks in shards:
        draws = jax.random.uniform(jax.random.fold_in(jax.random.fold_in(stream_key, 6), axis_at), (blocks,), jnp.float32, low / len(shards), high / len(shards))
        gain = gain * jnp.repeat(jnp.exp(draws), extent[axis_at] // blocks).reshape((-1,) + (1,) * (len(extent) - 1 - axis_at))
    return gain


def gaussian(own_key, extent, scale, most, pieces=(), kind=jnp.bfloat16):
    loudness = level_of(own_key, extent, pieces, -0.22, 0.18) if pieces else 1.0
    values = jax.random.normal(own_key, extent, jnp.float32) * scale * loudness
    return jnp.minimum(jnp.maximum(values, -most), most).astype(kind)


def setup_inputs(seed: int = 0) -> dict:
    key_list = jax.random.split(jax.random.key(seed), 7)
    gate_in = gaussian(key_list[0], (SECTIONS, TOKENS, CH), 1.0, 6.0, ((0, 4), (1, 16), (2, 8)))
    value_in = gaussian(key_list[1], (SECTIONS, TOKENS, CH), 1.0, 6.0, ((0, 4), (1, 16), (2, 8)))
    gate_out = gaussian(key_list[2], (SECTIONS, TOKENS, CH), 1.0, 6.0, ((0, 4), (1, 16), (2, 8)))
    filter_spectrum = draw_filter_spectrum(jax.random.fold_in(key_list[6], 71), 0)
    skip = gaussian(key_list[4], (SECTIONS, CH), 1.0, 4.0, ((0, 4), (1, 8)))
    out_weight = gaussian(key_list[5], (SECTIONS, CH, D), CH ** -0.5, 0.125, ((0, 4), (1, 16), (2, 8)))
    return dict(gate_in=gate_in, value_in=value_in, gate_out=gate_out, filter_spectrum=filter_spectrum, skip=skip, out_weight=out_weight)


def one_section(inputs):
    gate_a, value_a, gate_b, spectrum, skip_row, weight = inputs
    products = (gate_a.astype(jnp.float32) * value_a.astype(jnp.float32)).astype(jnp.bfloat16)
    values = products.astype(jnp.float32)
    length = 2 * TOKENS
    real_part = jnp.transpose(spectrum[:, 0].astype(jnp.float32), (1, 0, 2)).reshape(length, CH)
    imag_part = jnp.transpose(spectrum[:, 1].astype(jnp.float32), (1, 0, 2)).reshape(length, CH)
    response = real_part + 1j * imag_part
    transformed = jnp.fft.fft(values, n=length, axis=0)
    convolved = jnp.real(jnp.fft.ifft(transformed * response, axis=0))[:TOKENS].astype(jnp.float32)
    hidden = ((convolved + skip_row.astype(jnp.float32) * values) * gate_b.astype(jnp.float32)).astype(jnp.bfloat16)
    return jnp.dot(hidden, weight, preferred_element_type=jnp.float32).astype(jnp.bfloat16)


def reference(gate_in, value_in, gate_out, filter_spectrum, skip, out_weight):
    outputs = lax.map(one_section, (gate_in, value_in, gate_out, filter_spectrum, skip, out_weight))
    return jnp.roll(outputs, 1, axis=0)
```

```python
import functools
import math

import jax
import jax.numpy as jnp
import numpy as np
from jax import lax
from jax.experimental import pallas as pl
from jax.experimental.pallas import tpu as pltpu
from jax.sharding import PartitionSpec as P


def tables(rows, cols):
    total = rows * cols
    half = rows // 2
    k1 = np.arange(rows)
    angle = 2.0 * math.pi / rows * ((k1[:, None] * np.arange(half)[None, :]) % rows)
    first = np.concatenate([np.cos(angle), -np.sin(angle)], axis=0)
    s = np.arange(cols)
    angle = 2.0 * math.pi / cols * ((s[:, None] * s[None, :]) % cols)
    c, d = np.cos(angle), np.sin(angle)
    second = np.block([[c, -d], [d, c]])
    third = np.block([[c, d], [-d, c]])
    angle = 2.0 * math.pi / rows * ((np.arange(half)[:, None] * k1[None, :]) % rows)
    fourth = np.concatenate([np.cos(angle), -np.sin(angle)], axis=1) / total
    angle = 2.0 * math.pi / total * ((k1[:, None] * s[None, :]) % total)
    twist = np.stack([np.cos(angle), np.sin(angle)])
    cast = lambda m: jnp.asarray(m.astype(np.float32)).astype(jnp.bfloat16)
    return cast(first), cast(second), cast(third), cast(fourth), jnp.asarray(twist.astype(np.float32))


def conv_kernel(group, x_ref, f_ref, m1, m2, m3, m4, twist, o_ref):
    rows, cols = twist.shape[1:]
    dot = functools.partial(jnp.dot, preferred_element_type=jnp.float32)
    for c in range(group):
        tc, ts = twist[0], twist[1]
        y = dot(m1[...], x_ref[c])
        yr, yi = y[:rows], y[rows:]
        y = jnp.concatenate([yr * tc + yi * ts, yi * tc - yr * ts], axis=1)
        x = dot(y.astype(jnp.bfloat16), m2[...])
        xr, xi = x[:, :cols], x[:, cols:]
        hr = f_ref[c, :, :cols].astype(jnp.float32)
        hi = f_ref[c, :, cols:].astype(jnp.float32)
        z = jnp.concatenate([xr * hr - xi * hi, xr * hi + xi * hr], axis=1)
        v = dot(z.astype(jnp.bfloat16), m3[...])
        vr, vi = v[:, :cols], v[:, cols:]
        v = jnp.concatenate([vr * tc - vi * ts, vi * tc + vr * ts], axis=0)
        o_ref[c] = dot(m4[...], v.astype(jnp.bfloat16)).astype(o_ref.dtype)


def convolve(x, spectrum, group=2):
    chans, half, cols = x.shape
    rows = 2 * half
    consts = tables(rows, cols)
    whole = [pl.BlockSpec(c.shape, functools.partial(lambda n, i: (0,) * n, c.ndim)) for c in consts]
    return pl.pallas_call(
        functools.partial(conv_kernel, group),
        grid=(chans // group,),
        in_specs=[
            pl.BlockSpec((group, half, cols), lambda i: (i, 0, 0)),
            pl.BlockSpec((group, rows, 2 * cols), lambda i: (i, 0, 0)),
            *whole,
        ],
        out_specs=pl.BlockSpec((group, half, cols), lambda i: (i, 0, 0)),
        out_shape=jax.ShapeDtypeStruct(x.shape, jnp.bfloat16),
        cost_estimate=pl.CostEstimate(flops=2 * 800_000_000, bytes_accessed=6_000_000, transcendentals=0),
        compiler_params=pltpu.CompilerParams(vmem_limit_bytes=32 * 1024 * 1024),
    )(x, spectrum, *consts)


def per_device(gate_in, value_in, gate_out, filter_spectrum, skip, out_weight):
    products = (gate_in[0].astype(jnp.float32) * value_in[0].astype(jnp.float32)).astype(jnp.bfloat16)
    tok_count, chan_count = products.shape
    my_rows, _, cols, _ = filter_spectrum.shape[1:]
    spectrum = filter_spectrum[0].transpose(3, 0, 1, 2)
    spectrum = lax.all_to_all(spectrum, "ctx", split_axis=0, concat_axis=1, tiled=True)
    spectrum = spectrum.reshape(*spectrum.shape[:2], 2 * cols)
    x = products.reshape(tok_count // cols, cols, chan_count).transpose(2, 0, 1)
    x = lax.all_to_all(x, "ctx", split_axis=0, concat_axis=1, tiled=True)
    out = convolve(x, spectrum)
    out = lax.all_to_all(out, "ctx", split_axis=1, concat_axis=0, tiled=True)
    convolved = out.transpose(1, 2, 0).reshape(tok_count, chan_count).astype(jnp.float32)
    hidden = (
        (convolved + skip[0].astype(jnp.float32) * products.astype(jnp.float32))
        * gate_out[0].astype(jnp.float32)
    ).astype(jnp.bfloat16)
    count = lax.axis_size("section")
    pairs = [(source, (source + 1) % count) for source in range(count)]
    hidden = lax.ppermute(hidden, "section", pairs)
    weight = lax.ppermute(out_weight[0], "section", pairs)
    weight = lax.all_gather(weight, "ctx", axis=0, tiled=True)
    features = lax.all_gather(hidden, "tensor", axis=1, tiled=True)
    return jnp.dot(features, weight, preferred_element_type=jnp.float32).astype(jnp.bfloat16)[None]


def solution(mesh):
    placed = (
        P("section", "ctx", "tensor"),
        P("section", "ctx", "tensor"),
        P("section", "ctx", "tensor"),
        P("section", "ctx", None, None, "tensor"),
        P("section", "tensor"),
        P("section", "ctx", "tensor"),
    )
    return jax.shard_map(
        per_device,
        mesh=mesh,
        in_specs=placed,
        out_specs=P("section", "ctx", "tensor"),
        check_vma=False,
    )
```

```python
import functools
import math

import jax
import jax.numpy as jnp
import numpy as np
from jax import lax
from jax.experimental import pallas as pl
from jax.experimental.pallas import tpu as pltpu
from jax.sharding import PartitionSpec as P

CHUNKS = 2
MESH = pl.DeviceIdType.MESH


def tables(rows, cols, count):
    total = rows * cols
    half = rows // 2
    k1 = np.arange(rows)
    angle = 2.0 * math.pi / rows * ((k1[:, None] * np.arange(half)[None, :]) % rows)
    single = np.concatenate([np.cos(angle), -np.sin(angle)], axis=0)
    first = np.zeros((2, 2 * rows, count, 2, half // count))
    for c in range(2):
        first[c, :, :, c, :] = single.reshape(2 * rows, count, half // count)
    first = first.reshape(4 * rows, 2 * half)
    s = np.arange(cols)
    angle = 2.0 * math.pi / cols * ((s[:, None] * s[None, :]) % cols)
    c, d = np.cos(angle), np.sin(angle)
    second = np.block([[c, -d], [d, c]])
    third = np.block([[c, d], [-d, c]])
    angle = 2.0 * math.pi / rows * ((np.arange(half)[:, None] * k1[None, :]) % rows)
    fourth = np.concatenate([np.cos(angle), -np.sin(angle)], axis=1) / total
    angle = 2.0 * math.pi / total * ((k1[:, None] * s[None, :]) % total)
    twist = np.stack([np.cos(angle), np.sin(angle)])
    cast = lambda m: jnp.asarray(m.astype(np.float32)).astype(jnp.bfloat16)
    eye = cast(np.eye(cols))
    return cast(first), cast(second), cast(third), cast(fourth), jnp.asarray(twist.astype(np.float32)), eye


def dot(a, b):
    return jnp.dot(a, b, preferred_element_type=jnp.float32)


def kernel(
    n, nz, ns, sp, sf, gate, skip, w_ref, m1, m2, m3, m4, twist, eye, out,
    rp, rf, xs, so, ro, of, feat, wf, acc, gr,
    loc, p_sem, g_sem, f_sem, o_sem, wy_sem, wx_sem, ring_s, ring_r,
):
    me, z, sec = lax.axis_index("ctx"), lax.axis_index("tensor"), lax.axis_index("section")
    ny = math.isqrt(n)
    mx, my = me // ny, me % ny
    after, before = lax.rem(sec + 1, ns), lax.rem(sec + ns - 1, ns)
    zr, zl = lax.rem(z + 1, nz), lax.rem(z + nz - 1, nz)
    rows, cols = twist.shape[1:]
    pairs = rp.shape[1]
    own = pl.ds(pl.multiple_of(16 * me, 16), 16)

    barrier = pltpu.get_barrier_semaphore()

    @pl.loop(1, n)
    def _(i):
        pl.semaphore_signal(barrier, inc=1, device_id={"ctx": lax.rem(me + i, n)}, device_id_type=MESH)

    @pl.loop(0, n)
    def _(i):
        pl.semaphore_signal(
            barrier, inc=1, device_id={"section": before, "ctx": lax.rem(me + i, n)}, device_id_type=MESH
        )

    for zz in (zr, zl):
        pl.semaphore_signal(barrier, inc=1, device_id={"tensor": zz}, device_id_type=MESH)
    pl.semaphore_wait(barrier, 2 * n + 1)

    def remote(src, dst, send, recv, where):
        return pltpu.make_async_remote_copy(
            src_ref=src, dst_ref=dst, send_sem=send, recv_sem=recv, device_id=where, device_id_type=MESH
        )

    def send_p(i):
        d = lax.rem(me + i, n)
        return remote(sp.at[:, d], rp.at[:, :, own], p_sem.at[0], p_sem.at[1], {"ctx": d})

    def send_f(g, i):
        d = lax.rem(me + i, n)
        return remote(sf.at[g, d], rf.at[g, :, own], f_sem.at[g, 0], f_sem.at[g, 1], {"ctx": d})

    def send_o(g, i):
        d = lax.rem(me + i, n)
        return remote(so.at[g, d], ro.at[g, me], o_sem.at[g, 0], o_sem.at[g, 1], {"section": after, "ctx": d})

    def send_wy(i):
        d = mx * ny + lax.rem(my + i, ny)
        return remote(w_ref, wf.at[me], wy_sem.at[0], wy_sem.at[1], {"section": after, "ctx": d})

    mine_w = wf.at[pl.ds(mx * ny, ny)]

    def send_wx(i):
        d = lax.rem(mx + i, n // ny) * ny + my
        return remote(mine_w, mine_w, wx_sem.at[0], wx_sem.at[1], {"ctx": d})

    def wait_bytes(ref, sem):
        pltpu.make_async_copy(ref, ref, sem).wait()

    local = [pltpu.make_async_copy(sp.at[:, me], rp.at[:, :, own], loc.at[0])]
    for g in range(CHUNKS):
        local.append(pltpu.make_async_copy(sf.at[g, me], rf.at[g, :, own], loc.at[1 + g]))

    @pl.loop(1, n)
    def _(i):
        send_p(i).start()

    @pl.loop(1, n)
    def _(i):
        send_f(0, i).start()

    for copy in local:
        copy.start()

    @pl.loop(0, ny)
    def _(i):
        send_wy(i).start()

    send_gate = remote(gate, gr, g_sem.at[0], g_sem.at[1], {"section": after})
    send_gate.start()

    @pl.loop(1, n)
    def _(i):
        send_f(1, i).start()

    for copy in local:
        copy.wait()
    wait_bytes(rp.at[:, :, pl.ds(0, 16 * (n - 1))], p_sem.at[1])

    for g in range(CHUNKS):
        @pl.loop(0, pairs)
        def _(p, g=g):
            y = dot(m1[...], rp[g, p])
            for c in range(2):
                yr = y[2 * c * rows : (2 * c + 1) * rows]
                yi = y[(2 * c + 1) * rows : (2 * c + 2) * rows]
                t = jnp.concatenate([yr * twist[0] + yi * twist[1], yi * twist[0] - yr * twist[1]], axis=1)
                xs[g, 2 * p + c] = dot(t.astype(jnp.bfloat16), m2[...])

    wait_bytes(mine_w, wy_sem.at[1])

    @pl.loop(1, n // ny)
    def _(i):
        send_wx(i).start()

    def inverse(g):
        wait_bytes(rf.at[g, :, pl.ds(0, 16 * (n - 1))], f_sem.at[g, 1])

        @pl.loop(0, pairs)
        def _(p):
            made = []
            px = rp[g, p].astype(jnp.float32).reshape(n, 2, 8, cols)
            for c in range(2):
                x = xs[g, 2 * p + c]
                xr, xi = x[:, :cols], x[:, cols:]
                hr = rf[g, 2 * p + c, :, :cols].astype(jnp.float32)
                hi = rf[g, 2 * p + c, :, cols:].astype(jnp.float32)
                q = jnp.concatenate([xr * hr - xi * hi, xr * hi + xi * hr], axis=1)
                v = dot(q.astype(jnp.bfloat16), m3[...])
                vr, vi = v[:, :cols], v[:, cols:]
                v = jnp.concatenate([vr * twist[0] - vi * twist[1], vi * twist[0] + vr * twist[1]], axis=0)
                o = dot(m4[...], v.astype(jnp.bfloat16)).reshape(n, 1, 8, cols)
                made.append(o + px[:, c : c + 1] * skip[g, 2 * p + c].reshape(1, 1, 1, cols))
            both = jnp.concatenate(made, axis=1).reshape(n, 16, cols)
            so[g, :, p] = both.astype(jnp.bfloat16)

        @pl.loop(0, n)
        def _(i):
            send_o(g, i).start()

    def gating(g):
        wait_bytes(ro.at[g], o_sem.at[g, 1])
        of[...] = ro[g].reshape(of.shape).astype(jnp.float32)
        for r in range(8):
            block = of[pl.ds(r, cols, stride=8), :].astype(jnp.bfloat16)
            turned = lax.dot_general(eye[...], block, (((1,), (1,)), ((), ())), preferred_element_type=jnp.float32)
            tok = pl.ds(r * cols, cols)
            h = turned * gr[tok, g * cols : (g + 1) * cols].astype(jnp.float32)
            feat[g, z, tok, :] = h.astype(jnp.bfloat16)

    toks = feat.shape[2]
    far = nz // 2

    def ring(g, k, way):
        origin = lax.rem(z - k + nz, nz) if way == 0 else lax.rem(z + k, nz)
        ref = feat.at[g, origin]
        if k == far - 1:
            ref = ref.at[pl.ds(way * (toks // 2), toks // 2)]
        return remote(ref, ref, ring_s.at[g, way, k], ring_r.at[g, way, k], {"tensor": zr if way == 0 else zl})

    def ring_step(g, k):
        for way in range(2):
            if k > 0:
                ring(g, k - 1, way).wait_recv()
            if k < far:
                ring(g, k, way).start()

    def block_of(g, offsets, tok):
        where = [lax.rem(z + k + nz, nz) for k in offsets]
        left = jnp.concatenate([feat[g, o, tok, :] for o in where], axis=1)
        right = jnp.concatenate([wf[CHUNKS * o + g] for o in where], axis=0)
        return dot(left, right)

    tile = min(256, toks)

    def project(g, offsets, how):
        @pl.loop(0, toks // tile)
        def _(t):
            tok = pl.ds(pl.multiple_of(t * tile, tile), tile)
            value = block_of(g, offsets, tok)
            if how == "set":
                acc[tok, :] = value
            elif how == "add":
                acc[tok, :] += value
            else:
                out[tok, :] = (acc[tok, :] + value).astype(out.dtype)

    inverse(0)
    send_gate.wait_recv()
    gating(0)
    for k in range(far - 1):
        ring_step(0, k)
    inverse(1)
    for k in range(far - 1, far + 1):
        ring_step(0, k)
    gating(1)
    ring_step(1, 0)
    far_w = wf.at[pl.ds(0, n - ny)]
    wait_bytes(far_w, wx_sem.at[1])
    project(0, list(range(nz)), "set")
    for k in range(1, far):
        ring_step(1, k)
        project(1, [0] if k == 1 else [1 - k, k - 1], "add")
    ring_step(1, far)
    project(1, [1 - far, far - 1, far], "out")

    send_gate.wait_send()
    wait_bytes(sp.at[:, pl.ds(0, n - 1)], p_sem.at[0])
    for g in range(CHUNKS):
        wait_bytes(sf.at[g, pl.ds(0, n - 1)], f_sem.at[g, 0])
        wait_bytes(so.at[g], o_sem.at[g, 0])
        for way in range(2):
            for k in range(far):
                ring(g, k, way).wait_send()
    wait_bytes(mine_w, wy_sem.at[0])
    wait_bytes(far_w, wx_sem.at[0])


def per_device(gate_in, value_in, gate_out, filter_spectrum, skip, out_weight):
    n, nz, ns = lax.axis_size("ctx"), lax.axis_size("tensor"), lax.axis_size("section")
    products = (gate_in[0].astype(jnp.float32) * value_in[0].astype(jnp.float32)).astype(jnp.bfloat16)
    toks, chans = products.shape
    k1s, _, cols, _ = filter_spectrum.shape[1:]
    feats = out_weight.shape[2]
    rows = n * k1s
    each = chans // (n * CHUNKS)
    pairs = each // 2
    sf = filter_spectrum[0].transpose(3, 0, 1, 2).reshape(CHUNKS, n, each, k1s, 2 * cols)
    sp = products.reshape(toks // cols, cols, chans).transpose(2, 0, 1).reshape(CHUNKS, n, pairs, 16, cols)
    mine = skip[0].astype(jnp.float32).reshape(CHUNKS, n, each)
    mine = lax.dynamic_index_in_dim(mine, lax.axis_index("ctx"), axis=1, keepdims=False)
    mine = jnp.broadcast_to(mine[:, :, None, None], (CHUNKS, each, 1, cols))
    consts = tables(rows, cols, n)
    vmem = pl.BlockSpec(memory_space=pltpu.VMEM)
    bf, f32 = jnp.bfloat16, jnp.float32
    dma = pltpu.SemaphoreType.DMA
    out = pl.pallas_call(
        functools.partial(kernel, n, nz, ns),
        out_shape=jax.ShapeDtypeStruct((toks, feats), bf),
        in_specs=[vmem] * (5 + len(consts)),
        out_specs=vmem,
        scratch_shapes=[
            pltpu.VMEM((CHUNKS, pairs, 16 * n, cols), bf),
            pltpu.VMEM((CHUNKS, each, rows, 2 * cols), bf),
            pltpu.VMEM((CHUNKS, each, rows, 2 * cols), f32),
            pltpu.VMEM((CHUNKS, n, pairs, 16, cols), bf),
            pltpu.VMEM((CHUNKS, n, pairs, 16, cols), bf),
            pltpu.VMEM((n * pairs * 16, cols), f32),
            pltpu.VMEM((CHUNKS, nz, toks, chans // CHUNKS), bf),
            pltpu.VMEM((n, *out_weight.shape[1:]), bf),
            pltpu.VMEM((toks, feats), f32),
            pltpu.VMEM((toks, chans), bf),
            dma((1 + CHUNKS,)),
            dma((2,)),
            dma((2,)),
            dma((CHUNKS, 2)),
            dma((CHUNKS, 2)),
            dma((2,)),
            dma((2,)),
            dma((CHUNKS, 2, nz // 2)),
            dma((CHUNKS, 2, nz // 2)),
        ],
        cost_estimate=pl.CostEstimate(flops=6_000_000_000, bytes_accessed=8_000_000, transcendentals=0),
        compiler_params=pltpu.CompilerParams(
            collective_id=0, has_side_effects=True, vmem_limit_bytes=56 * 1024 * 1024
        ),
    )(sp, sf, gate_out[0], mine, out_weight[0], *consts)
    return out[None]


def solution(mesh):
    placed = (
        P("section", "ctx", "tensor"),
        P("section", "ctx", "tensor"),
        P("section", "ctx", "tensor"),
        P("section", "ctx", None, None, "tensor"),
        P("section", "tensor"),
        P("section", "ctx", "tensor"),
    )
    return jax.shard_map(
        per_device,
        mesh=mesh,
        in_specs=placed,
        out_specs=P("section", "ctx", "tensor"),
        check_vma=False,
    )
```

```python
import functools
import math

import jax
import jax.numpy as jnp
import numpy as np
from jax import lax
from jax.experimental import pallas as pl
from jax.experimental.pallas import tpu as pltpu
from jax.sharding import PartitionSpec as P

CHUNKS = 4
PIECES = 4
MESH = pl.DeviceIdType.MESH


def tables(rows, cols, count):
    total = rows * cols
    half = rows // 2
    k1 = np.arange(rows)
    angle = 2.0 * math.pi / rows * ((k1[:, None] * np.arange(half)[None, :]) % rows)
    single = np.concatenate([np.cos(angle), -np.sin(angle)], axis=0)
    first = np.zeros((2, 2 * rows, count, 2, half // count))
    for c in range(2):
        first[c, :, :, c, :] = single.reshape(2 * rows, count, half // count)
    first = first.reshape(4 * rows, 2 * half)
    s = np.arange(cols)
    angle = 2.0 * math.pi / cols * ((s[:, None] * s[None, :]) % cols)
    c, d = np.cos(angle), np.sin(angle)
    second = np.block([[c, -d], [d, c]])
    third = np.block([[c, d], [-d, c]])
    angle = 2.0 * math.pi / rows * ((np.arange(half)[:, None] * k1[None, :]) % rows)
    fourth = np.concatenate([np.cos(angle), -np.sin(angle)], axis=1) / total
    angle = 2.0 * math.pi / total * ((k1[:, None] * s[None, :]) % total)
    twist = np.stack([np.cos(angle), np.sin(angle)])
    cast = lambda m: jnp.asarray(m.astype(np.float32)).astype(jnp.bfloat16)
    eye = cast(np.eye(cols))
    return cast(first), cast(second), cast(third), cast(fourth), jnp.asarray(twist.astype(np.float32)), eye


def dot(a, b):
    return jnp.dot(a, b, preferred_element_type=jnp.float32)


def turn(eye, block):
    return lax.dot_general(eye, block, (((1,), (1,)), ((), ())), preferred_element_type=jnp.float32)


def kernel(
    n, nz, ns, gate_in, value_in, f_ref, gate, skip, w_ref, m1, m2, m3, m4, twist, eye, out,
    f_in, wide, sp, sf, rp, rf, xs, so, ro, feat, wf, acc, gr,
    loc, p_sem, g_sem, f_sem, o_sem, wy_sem, wx_sem, ring_s, ring_r,
):
    me, z, sec = lax.axis_index("ctx"), lax.axis_index("tensor"), lax.axis_index("section")
    ny = math.isqrt(n)
    mx, my = me // ny, me % ny
    after, before = lax.rem(sec + 1, ns), lax.rem(sec + ns - 1, ns)
    zr, zl = lax.rem(z + 1, nz), lax.rem(z + nz - 1, nz)
    rows, cols = twist.shape[1:]
    pairs = rp.shape[1]
    each = 2 * pairs
    chans = gate_in.shape[1]
    width = chans // CHUNKS
    own = pl.ds(pl.multiple_of(16 * me, 16), 16)

    load_f = pltpu.make_async_copy(f_ref, f_in, loc.at[0])
    load_f.start()
    barrier = pltpu.get_barrier_semaphore()

    @pl.loop(1, n)
    def _(i):
        pl.semaphore_signal(barrier, inc=1, device_id={"ctx": lax.rem(me + i, n)}, device_id_type=MESH)

    @pl.loop(0, n)
    def _(i):
        pl.semaphore_signal(
            barrier, inc=1, device_id={"section": before, "ctx": lax.rem(me + i, n)}, device_id_type=MESH
        )

    for zz in (zr, zl):
        pl.semaphore_signal(barrier, inc=1, device_id={"tensor": zz}, device_id_type=MESH)

    for r in range(8):
        tok = slice(r * cols, (r + 1) * cols)
        for h in range(chans // cols):
            lanes = slice(h * cols, (h + 1) * cols)
            prod = gate_in[tok, lanes].astype(jnp.float32) * value_in[tok, lanes].astype(jnp.float32)
            wide[0, pl.ds(h * cols * 8 + r, cols, stride=8), :] = turn(eye[...], prod.astype(jnp.bfloat16))
    part = 8 * chans // CHUNKS
    for g in range(CHUNKS):
        block = wide[0, g * part : (g + 1) * part, :].astype(jnp.bfloat16)
        sp[g] = block.reshape(n, pairs, 16, cols)

    pl.semaphore_wait(barrier, 2 * n + 1)

    def remote(src, dst, send, recv, where):
        return pltpu.make_async_remote_copy(
            src_ref=src, dst_ref=dst, send_sem=send, recv_sem=recv, device_id=where, device_id_type=MESH
        )

    def send_p(i):
        d = lax.rem(me + i, n)
        return remote(sp.at[:, d], rp.at[:, :, own], p_sem.at[0], p_sem.at[1], {"ctx": d})

    def send_f(g, i):
        d = lax.rem(me + i, n)
        return remote(sf.at[g, d], rf.at[g, :, own], f_sem.at[g, 0], f_sem.at[g, 1], {"ctx": d})

    def send_o(g, i):
        d = lax.rem(me + i, n)
        return remote(so.at[g, d], ro.at[g, me], o_sem.at[g, 0], o_sem.at[g, 1], {"section": after, "ctx": d})

    def send_wy(i):
        d = mx * ny + lax.rem(my + i, ny)
        return remote(w_ref, wf.at[me], wy_sem.at[0], wy_sem.at[1], {"section": after, "ctx": d})

    mine_w = wf.at[pl.ds(mx * ny, ny)]
    far_w = wf.at[pl.ds(0, n - ny)]

    def send_wx(i):
        d = lax.rem(mx + i, n // ny) * ny + my
        return remote(mine_w, mine_w, wx_sem.at[0], wx_sem.at[1], {"ctx": d})

    def wait_bytes(ref, sem):
        pltpu.make_async_copy(ref, ref, sem).wait()

    def start_all(copy, first, last):
        @pl.loop(first, last)
        def _(i):
            copy(i).start()

    own_p = pltpu.make_async_copy(sp.at[:, me], rp.at[:, :, own], loc.at[1])

    def own_f(g):
        return pltpu.make_async_copy(sf.at[g, me], rf.at[g, :, own], loc.at[2 + g])

    start_all(send_p, 1, n)
    own_p.start()

    def turn_spectrum(h):
        for k in range(16):
            block = f_in[k, :, :, h * cols : (h + 1) * cols].reshape(2 * cols, cols)
            turned = turn(eye[...], block)
            for c in range(2):
                wide[c, pl.ds(k, cols, stride=16), :] = turned[:, c * cols : (c + 1) * cols]
        for g in range(2):
            size = 8 * cols
            block = jnp.concatenate([wide[c, g * size : (g + 1) * size, :] for c in range(2)], axis=1).astype(jnp.bfloat16)
            sf[2 * h + g] = block.reshape(n, each, 16, 2 * cols)
            own_f(2 * h + g).start()

    def start_f(g):
        start_all(functools.partial(send_f, g), 1, n)

    def sent_f(g):
        wait_bytes(sf.at[g, pl.ds(0, n - 1)], f_sem.at[g, 0])

    load_f.wait()
    turn_spectrum(0)
    start_f(0)
    send_gate = remote(gate, gr, g_sem.at[0], g_sem.at[1], {"section": after})
    send_gate.start()
    start_all(send_wy, 0, ny)
    turn_spectrum(1)

    own_p.wait()
    wait_bytes(rp.at[:, :, pl.ds(0, 16 * (n - 1))], p_sem.at[1])

    for g in range(CHUNKS):
        @pl.loop(0, pairs)
        def _(p, g=g):
            y = dot(m1[...], rp[g, p])
            for c in range(2):
                yr = y[2 * c * rows : (2 * c + 1) * rows]
                yi = y[(2 * c + 1) * rows : (2 * c + 2) * rows]
                t = jnp.concatenate([yr * twist[0] + yi * twist[1], yi * twist[0] - yr * twist[1]], axis=1)
                xs[g, 2 * p + c] = dot(t.astype(jnp.bfloat16), m2[...])

    def inverse(g):
        own_f(g).wait()
        wait_bytes(rf.at[g, :, pl.ds(0, 16 * (n - 1))], f_sem.at[g, 1])

        @pl.loop(0, pairs)
        def _(p):
            made = []
            px = rp[g, p].astype(jnp.float32).reshape(n, 2, 8, cols)
            for c in range(2):
                x = xs[g, 2 * p + c]
                xr, xi = x[:, :cols], x[:, cols:]
                hr = rf[g, 2 * p + c, :, :cols].astype(jnp.float32)
                hi = rf[g, 2 * p + c, :, cols:].astype(jnp.float32)
                q = jnp.concatenate([xr * hr - xi * hi, xr * hi + xi * hr], axis=1)
                v = dot(q.astype(jnp.bfloat16), m3[...])
                vr, vi = v[:, :cols], v[:, cols:]
                v = jnp.concatenate([vr * twist[0] - vi * twist[1], vi * twist[0] + vr * twist[1]], axis=0)
                o = dot(m4[...], v.astype(jnp.bfloat16)).reshape(n, 1, 8, cols)
                made.append(o + px[:, c : c + 1] * skip[0, g * width + each * me + 2 * p + c])
            both = jnp.concatenate(made, axis=1).reshape(n, 16, cols)
            so[g, :, p] = both.astype(jnp.bfloat16)

        start_all(functools.partial(send_o, g), 0, n)

    lane = lax.broadcasted_iota(jnp.int32, (cols, cols), 1)

    def gating(g):
        wait_bytes(ro.at[g], o_sem.at[g, 1])
        wide[0, 0 : 8 * width, :] = ro[g].reshape(8 * width, cols).astype(jnp.float32)
        lanes = slice(g // 2 * cols, (g // 2 + 1) * cols)
        for r in range(4):
            picked = [wide[0, pl.ds(k, width, stride=8), :] for k in (r, r + 4)]
            low = gr[r * cols : (r + 1) * cols, lanes].astype(jnp.float32)
            high = gr[(r + 4) * cols : (r + 5) * cols, lanes].astype(jnp.float32)
            high = pltpu.roll(high, width, 1)
            if g % 2 == 1:
                picked = picked[::-1]
                by = jnp.where(lane < width, high, low)
            else:
                by = jnp.where(lane < width, low, high)
            turned = turn(eye[...], jnp.concatenate(picked, axis=0).astype(jnp.bfloat16))
            feat[g, z, r * cols : (r + 1) * cols, :] = (turned * by).astype(jnp.bfloat16)

    toks = feat.shape[2]
    far = nz // 2

    def ring(g, k, way, piece):
        origin = lax.rem(z - k + nz, nz) if way == 0 else lax.rem(z + k, nz)
        size = toks // PIECES
        first = piece * size
        if k == far - 1:
            size = size // 2
            first = way * (toks // 2) + piece * size
        ref = feat.at[g, origin, pl.ds(first, size)]
        where = {"tensor": zr if way == 0 else zl}
        return remote(ref, ref, ring_s.at[g, way, k, piece], ring_r.at[g, way, k, piece], where)

    def arrived(g, k, way, piece):
        if k == far - 1:
            half = PIECES // 2
            if piece % 2 == 0:
                for p in range(half * way + piece // 2, half * way + piece // 2 + 1):
                    ring(g, k - 1, way, p).wait_recv()
        else:
            ring(g, k - 1, way, piece).wait_recv()

    def ring_step(g, k):
        for piece in range(PIECES):
            for way in range(2):
                if k > 0:
                    arrived(g, k, way, piece)
                if k < far:
                    ring(g, k, way, piece).start()
        if k == far - 1:
            for way in range(2):
                for p in range(PIECES // 2):
                    ring(g, k - 1, way, (1 - way) * (PIECES // 2) + p).wait_recv()

    tile = min(128, toks)
    tile_lane = lax.broadcasted_iota(jnp.int32, (tile, cols), 1)

    def project(h, offsets, how):
        where = [lax.rem(z + k + nz, nz) for k in offsets]

        @pl.loop(0, toks // tile)
        def _(t):
            tok = pl.ds(pl.multiple_of(t * tile, tile), tile)
            even = [feat[2 * h, o, tok, :] for o in where]
            odd = [feat[2 * h + 1, o, tok, :] for o in where]
            for half in range(2):
                first, second = (even, odd) if half == 0 else (odd, even)
                left = jnp.concatenate([jnp.where(tile_lane < width, a, b) for a, b in zip(first, second)], axis=1)
                right = []
                for o in where:
                    w = wf[2 * o + h]
                    right += [w] if half == 0 else [w[width:], w[:width]]
                value = dot(left, jnp.concatenate(right, axis=0))
                to = pl.ds(pl.multiple_of(half * toks + t * tile, tile), tile)
                if how == "set":
                    acc[to, :] = value
                elif how == "add":
                    acc[to, :] += value
                else:
                    out[to, :] = (acc[to, :] + value).astype(out.dtype)

    for g in range(CHUNKS):
        if g == 0:
            sent_f(0)
            start_f(1)
        inverse(g)
        if g == 0:
            wait_bytes(mine_w, wy_sem.at[1])
            start_all(send_wx, 1, n // ny)
            send_gate.wait_recv()
        else:
            for k in range(2, far):
                ring_step(g - 1, k)
        gating(g)
        ring_step(g, 0)
        if g + 2 < CHUNKS:
            sent_f(g + 1)
            start_f(g + 2)
        if g > 0:
            ring_step(g - 1, far)
        if g == 2:
            wait_bytes(far_w, wx_sem.at[1])
            project(0, list(range(nz)), "set")
        ring_step(g, 1)
    last = CHUNKS - 1
    project(1, [0], "add")
    for k in range(2, far):
        ring_step(last, k)
        project(1, [1 - k, k - 1], "add")
    ring_step(last, far)
    project(1, [1 - far, far - 1, far], "out")

    send_gate.wait_send()
    wait_bytes(sp.at[:, pl.ds(0, n - 1)], p_sem.at[0])
    for g in range(CHUNKS):
        if g == CHUNKS - 1:
            sent_f(g)
        wait_bytes(so.at[g], o_sem.at[g, 0])
        for way in range(2):
            for k in range(far):
                for piece in range(PIECES):
                    ring(g, k, way, piece).wait_send()
    wait_bytes(mine_w, wy_sem.at[0])
    wait_bytes(far_w, wx_sem.at[0])


def per_device(gate_in, value_in, gate_out, filter_spectrum, skip, out_weight):
    n, nz, ns = lax.axis_size("ctx"), lax.axis_size("tensor"), lax.axis_size("section")
    toks, chans = gate_in.shape[1:]
    k1s, _, cols, _ = filter_spectrum.shape[1:]
    feats = out_weight.shape[2]
    rows = n * k1s
    each = chans // (n * CHUNKS)
    pairs = each // 2
    consts = tables(rows, cols, n)
    vmem = pl.BlockSpec(memory_space=pltpu.VMEM)
    anywhere = pl.BlockSpec(memory_space=pl.ANY)
    bf, f32 = jnp.bfloat16, jnp.float32
    dma = pltpu.SemaphoreType.DMA
    out = pl.pallas_call(
        functools.partial(kernel, n, nz, ns),
        out_shape=jax.ShapeDtypeStruct((toks, feats), bf),
        in_specs=[vmem, vmem, anywhere, anywhere, pl.BlockSpec(memory_space=pltpu.SMEM), anywhere] + [vmem] * len(consts),
        out_specs=vmem,
        scratch_shapes=[
            pltpu.VMEM((k1s, 2, cols, chans), bf),
            pltpu.VMEM((2, 16 * cols, cols), f32),
            pltpu.VMEM((CHUNKS, n, pairs, 16, cols), bf),
            pltpu.VMEM((CHUNKS, n, each, 16, 2 * cols), bf),
            pltpu.VMEM((CHUNKS, pairs, 16 * n, cols), bf),
            pltpu.VMEM((CHUNKS, each, rows, 2 * cols), bf),
            pltpu.VMEM((CHUNKS, each, rows, 2 * cols), f32),
            pltpu.VMEM((CHUNKS, n, pairs, 16, cols), bf),
            pltpu.VMEM((CHUNKS, n, pairs, 16, cols), bf),
            pltpu.VMEM((CHUNKS, nz, toks // 2, cols), bf),
            pltpu.VMEM((n, *out_weight.shape[1:]), bf),
            pltpu.VMEM((toks, feats), f32),
            pltpu.VMEM((toks, chans), bf),
            dma((2 + CHUNKS,)),
            dma((2,)),
            dma((2,)),
            dma((CHUNKS, 2)),
            dma((CHUNKS, 2)),
            dma((2,)),
            dma((2,)),
            dma((CHUNKS, 2, nz // 2, PIECES)),
            dma((CHUNKS, 2, nz // 2, PIECES)),
        ],
        cost_estimate=pl.CostEstimate(flops=6_000_000_000, bytes_accessed=8_000_000, transcendentals=0),
        compiler_params=pltpu.CompilerParams(
            collective_id=0, has_side_effects=True, vmem_limit_bytes=56 * 1024 * 1024
        ),
    )(gate_in[0], value_in[0], filter_spectrum[0], gate_out[0], skip.astype(f32), out_weight[0], *consts)
    return out[None]


def solution(mesh):
    placed = (
        P("section", "ctx", "tensor"),
        P("section", "ctx", "tensor"),
        P("section", "ctx", "tensor"),
        P("section", "ctx", None, None, "tensor"),
        P("section", "tensor"),
        P("section", "ctx", "tensor"),
    )
    return jax.shard_map(
        per_device,
        mesh=mesh,
        in_specs=placed,
        out_specs=P("section", "ctx", "tensor"),
        check_vma=False,
    )
```

```python
import functools
import math

import jax
import jax.numpy as jnp
import numpy as np
from jax import lax
from jax.experimental import pallas as pl
from jax.experimental.pallas import tpu as pltpu
from jax.sharding import PartitionSpec as P

CHUNKS = 4
PIECES = 2
MESH = pl.DeviceIdType.MESH


def tables(rows, cols, count):
    total = rows * cols
    half = rows // 2
    k1 = np.arange(rows)
    angle = 2.0 * math.pi / rows * ((k1[:, None] * np.arange(half)[None, :]) % rows)
    single = np.concatenate([np.cos(angle), -np.sin(angle)], axis=0)
    first = np.zeros((2, 2 * rows, count, 2, half // count))
    for c in range(2):
        first[c, :, :, c, :] = single.reshape(2 * rows, count, half // count)
    first = first.reshape(4 * rows, 2 * half)
    s = np.arange(cols)
    angle = 2.0 * math.pi / cols * ((s[:, None] * s[None, :]) % cols)
    c, d = np.cos(angle), np.sin(angle)
    second = np.block([[c, -d], [d, c]])
    third = np.block([[c, d], [-d, c]])
    angle = 2.0 * math.pi / rows * ((np.arange(half)[:, None] * k1[None, :]) % rows)
    fourth = np.concatenate([np.cos(angle), -np.sin(angle)], axis=1) / total
    angle = 2.0 * math.pi / total * ((k1[:, None] * s[None, :]) % total)
    twist = np.stack([np.cos(angle), np.sin(angle)])
    cast = lambda m: jnp.asarray(m.astype(np.float32)).astype(jnp.bfloat16)
    eye = cast(np.eye(cols))
    return cast(first), cast(second), cast(third), cast(fourth), jnp.asarray(twist.astype(np.float32)), eye


def dot(a, b):
    return jnp.dot(a, b, preferred_element_type=jnp.float32)


def turn(eye, block):
    return lax.dot_general(eye, block, (((1,), (1,)), ((), ())), preferred_element_type=jnp.float32)


def kernel(
    n, nz, ns, gate_any, value_any, f_ref, gate, skip, w_ref, m1_any, m2_any, m3_any, m4_any, twist_any, eye_any, out,
    f_in, wide, sp, sf, rp, rf, xs, so, ro, feat, wf, acc, gr,
    gate_in, value_in, eye, m1, m2, m3, m4, twist,
    loc, p_sem, g_sem, f_sem, o_sem, wy_sem, wx_sem, ring_s, ring_r, in_sem,
):
    me, z, sec = lax.axis_index("ctx"), lax.axis_index("tensor"), lax.axis_index("section")
    ny = math.isqrt(n)
    mx, my = me // ny, me % ny
    after, before = lax.rem(sec + 1, ns), lax.rem(sec + ns - 1, ns)
    zr, zl = lax.rem(z + 1, nz), lax.rem(z + nz - 1, nz)
    rows, cols = twist.shape[1:]
    pairs = rp.shape[1]
    each = 2 * pairs
    chans = gate_in.shape[1]
    width = chans // CHUNKS
    own = pl.ds(pl.multiple_of(16 * me, 16), 16)

    load_f = pltpu.make_async_copy(f_ref, f_in, loc.at[0])
    pulled = ((eye_any, eye), (gate_any, gate_in), (value_any, value_in), (m1_any, m1), (m2_any, m2), (m3_any, m3),
              (m4_any, m4), (twist_any, twist))
    loads = [pltpu.make_async_copy(src, dst, in_sem.at[k]) for k, (src, dst) in enumerate(pulled)]
    for k in range(3):
        loads[k].start()
    load_f.start()
    for k in range(3, len(loads)):
        loads[k].start()
    barrier = pltpu.get_barrier_semaphore()

    @pl.loop(1, n)
    def _(i):
        pl.semaphore_signal(barrier, inc=1, device_id={"ctx": lax.rem(me + i, n)}, device_id_type=MESH)

    @pl.loop(0, n)
    def _(i):
        pl.semaphore_signal(
            barrier, inc=1, device_id={"section": before, "ctx": lax.rem(me + i, n)}, device_id_type=MESH
        )

    for zz in (zr, zl):
        pl.semaphore_signal(barrier, inc=1, device_id={"tensor": zz}, device_id_type=MESH)

    for k in range(3):
        loads[k].wait()
    for r in range(8):
        tok = slice(r * cols, (r + 1) * cols)
        for h in range(chans // cols):
            lanes = slice(h * cols, (h + 1) * cols)
            prod = gate_in[tok, lanes].astype(jnp.float32) * value_in[tok, lanes].astype(jnp.float32)
            wide[0, pl.ds(h * cols * 8 + r, cols, stride=8), :] = turn(eye[...], prod.astype(jnp.bfloat16))
    part = 8 * chans // CHUNKS
    for g in range(CHUNKS):
        block = wide[0, g * part : (g + 1) * part, :].astype(jnp.bfloat16)
        sp[g] = block.reshape(n, pairs, 16, cols)

    pl.semaphore_wait(barrier, 2 * n + 1)

    def remote(src, dst, send, recv, where):
        return pltpu.make_async_remote_copy(
            src_ref=src, dst_ref=dst, send_sem=send, recv_sem=recv, device_id=where, device_id_type=MESH
        )

    def send_p(i):
        d = lax.rem(me + i, n)
        return remote(sp.at[:, d], rp.at[:, :, own], p_sem.at[0], p_sem.at[1], {"ctx": d})

    def send_f(g, i):
        d = lax.rem(me + i, n)
        return remote(sf.at[g, d], rf.at[g, :, own], f_sem.at[g, 0], f_sem.at[g, 1], {"ctx": d})

    def send_o(g, i):
        d = lax.rem(me + i, n)
        return remote(so.at[g, d], ro.at[g, me], o_sem.at[g, 0], o_sem.at[g, 1], {"section": after, "ctx": d})

    def send_wy(i):
        d = mx * ny + lax.rem(my + i, ny)
        return remote(w_ref, wf.at[me], wy_sem.at[0], wy_sem.at[1], {"section": after, "ctx": d})

    mine_w = wf.at[pl.ds(mx * ny, ny)]
    far_w = wf.at[pl.ds(0, n - ny)]

    def send_wx(i):
        d = lax.rem(mx + i, n // ny) * ny + my
        return remote(mine_w, mine_w, wx_sem.at[0], wx_sem.at[1], {"ctx": d})

    def wait_bytes(ref, sem):
        pltpu.make_async_copy(ref, ref, sem).wait()

    def start_all(copy, first, last):
        @pl.loop(first, last)
        def _(i):
            copy(i).start()

    own_p = pltpu.make_async_copy(sp.at[:, me], rp.at[:, :, own], loc.at[1])

    def own_f(g):
        return pltpu.make_async_copy(sf.at[g, me], rf.at[g, :, own], loc.at[2 + g])

    start_all(send_p, 1, n)
    own_p.start()

    def turn_spectrum(h):
        for k in range(16):
            block = f_in[k, :, :, h * cols : (h + 1) * cols].reshape(2 * cols, cols)
            turned = turn(eye[...], block)
            for c in range(2):
                wide[c, pl.ds(k, cols, stride=16), :] = turned[:, c * cols : (c + 1) * cols]
        for g in range(2):
            size = 8 * cols
            block = jnp.concatenate([wide[c, g * size : (g + 1) * size, :] for c in range(2)], axis=1).astype(jnp.bfloat16)
            sf[2 * h + g] = block.reshape(n, each, 16, 2 * cols)
            own_f(2 * h + g).start()

    def start_f(g):
        start_all(functools.partial(send_f, g), 1, n)

    def sent_f(g):
        wait_bytes(sf.at[g, pl.ds(0, n - 1)], f_sem.at[g, 0])

    load_f.wait()
    turn_spectrum(0)
    start_f(0)
    send_gate = remote(gate, gr, g_sem.at[0], g_sem.at[1], {"section": after})
    send_gate.start()
    start_all(send_wy, 0, ny)
    turn_spectrum(1)

    for k in range(3, len(loads)):
        loads[k].wait()
    own_p.wait()
    wait_bytes(rp.at[:, :, pl.ds(0, 16 * (n - 1))], p_sem.at[1])

    for g in range(CHUNKS):
        @pl.loop(0, pairs)
        def _(p, g=g):
            y = dot(m1[...], rp[g, p])
            for c in range(2):
                yr = y[2 * c * rows : (2 * c + 1) * rows]
                yi = y[(2 * c + 1) * rows : (2 * c + 2) * rows]
                t = jnp.concatenate([yr * twist[0] + yi * twist[1], yi * twist[0] - yr * twist[1]], axis=1)
                xs[g, 2 * p + c] = dot(t.astype(jnp.bfloat16), m2[...])

    def inverse(g):
        own_f(g).wait()
        wait_bytes(rf.at[g, :, pl.ds(0, 16 * (n - 1))], f_sem.at[g, 1])

        @pl.loop(0, pairs)
        def _(p):
            made = []
            px = rp[g, p].astype(jnp.float32).reshape(n, 2, 8, cols)
            for c in range(2):
                x = xs[g, 2 * p + c]
                xr, xi = x[:, :cols], x[:, cols:]
                hr = rf[g, 2 * p + c, :, :cols].astype(jnp.float32)
                hi = rf[g, 2 * p + c, :, cols:].astype(jnp.float32)
                q = jnp.concatenate([xr * hr - xi * hi, xr * hi + xi * hr], axis=1)
                v = dot(q.astype(jnp.bfloat16), m3[...])
                vr, vi = v[:, :cols], v[:, cols:]
                v = jnp.concatenate([vr * twist[0] - vi * twist[1], vi * twist[0] + vr * twist[1]], axis=0)
                o = dot(m4[...], v.astype(jnp.bfloat16)).reshape(n, 1, 8, cols)
                made.append(o + px[:, c : c + 1] * skip[0, g * width + each * me + 2 * p + c])
            both = jnp.concatenate(made, axis=1).reshape(n, 16, cols)
            so[g, :, p] = both.astype(jnp.bfloat16)

        start_all(functools.partial(send_o, g), 0, n)

    lane = lax.broadcasted_iota(jnp.int32, (cols, cols), 1)

    def gating(g):
        wait_bytes(ro.at[g], o_sem.at[g, 1])
        wide[0, 0 : 8 * width, :] = ro[g].reshape(8 * width, cols).astype(jnp.float32)
        lanes = slice(g // 2 * cols, (g // 2 + 1) * cols)
        for r in range(4):
            picked = [wide[0, pl.ds(k, width, stride=8), :] for k in (r, r + 4)]
            low = gr[r * cols : (r + 1) * cols, lanes].astype(jnp.float32)
            high = gr[(r + 4) * cols : (r + 5) * cols, lanes].astype(jnp.float32)
            high = pltpu.roll(high, width, 1)
            if g % 2 == 1:
                picked = picked[::-1]
                by = jnp.where(lane < width, high, low)
            else:
                by = jnp.where(lane < width, low, high)
            turned = turn(eye[...], jnp.concatenate(picked, axis=0).astype(jnp.bfloat16))
            feat[g, z, r * cols : (r + 1) * cols, :] = (turned * by).astype(jnp.bfloat16)

    toks = feat.shape[2]
    far = nz // 2

    def ring(g, k, way, piece):
        origin = lax.rem(z - k + nz, nz) if way == 0 else lax.rem(z + k, nz)
        size = toks // PIECES
        first = piece * size
        if k == far - 1:
            size = size // 2
            first = way * (toks // 2) + piece * size
        ref = feat.at[g, origin, pl.ds(first, size)]
        where = {"tensor": zr if way == 0 else zl}
        return remote(ref, ref, ring_s.at[g, way, k, piece], ring_r.at[g, way, k, piece], where)

    def arrived(g, k, way, piece):
        if k == far - 1:
            half = PIECES // 2
            if piece % 2 == 0:
                for p in range(half * way + piece // 2, half * way + piece // 2 + 1):
                    ring(g, k - 1, way, p).wait_recv()
        else:
            ring(g, k - 1, way, piece).wait_recv()

    def ring_step(g, k):
        for piece in range(PIECES):
            for way in range(2):
                if k > 0:
                    arrived(g, k, way, piece)
                if k < far:
                    ring(g, k, way, piece).start()
        if k == far - 1:
            for way in range(2):
                for p in range(PIECES // 2):
                    ring(g, k - 1, way, (1 - way) * (PIECES // 2) + p).wait_recv()

    tile = min(128, toks)
    tile_lane = lax.broadcasted_iota(jnp.int32, (tile, cols), 1)

    def project(h, offsets, how):
        where = [lax.rem(z + k + nz, nz) for k in offsets]

        @pl.loop(0, toks // tile)
        def _(t):
            tok = pl.ds(pl.multiple_of(t * tile, tile), tile)
            even = [feat[2 * h, o, tok, :] for o in where]
            odd = [feat[2 * h + 1, o, tok, :] for o in where]
            for half in range(2):
                first, second = (even, odd) if half == 0 else (odd, even)
                left = jnp.concatenate([jnp.where(tile_lane < width, a, b) for a, b in zip(first, second)], axis=1)
                right = []
                for o in where:
                    w = wf[2 * o + h]
                    right += [w] if half == 0 else [w[width:], w[:width]]
                value = dot(left, jnp.concatenate(right, axis=0))
                to = pl.ds(pl.multiple_of(half * toks + t * tile, tile), tile)
                if how == "set":
                    acc[to, :] = value
                elif how == "add":
                    acc[to, :] += value
                else:
                    out[to, :] = (acc[to, :] + value).astype(out.dtype)

    sent_f(0)
    start_f(1)
    last = CHUNKS - 1
    for g in range(CHUNKS):
        inverse(g)
        if g == 0:
            wait_bytes(mine_w, wy_sem.at[1])
            start_all(send_wx, 1, n // ny)
            send_gate.wait_recv()
        else:
            for k in range(2, far - 1):
                ring_step(g - 1, k)
        gating(g)
        ring_step(g, 0)
        if g + 2 < CHUNKS:
            start_f(g + 2)
        if g > 0:
            ring_step(g - 1, far - 1)
        if far > 2 or g == last:
            ring_step(g, 1)
        if g > 1:
            ring_step(g - 2, far)
    wait_bytes(far_w, wx_sem.at[1])
    project(0, list(range(nz)), "set")
    for k in range(2, far):
        ring_step(last, k)
        if k == 2:
            ring_step(last - 1, far)
            project(1, [0], "add")
        project(1, [1 - k, k - 1], "add")
    if far == 2:
        ring_step(last - 1, far)
    ring_step(last, far)
    project(1, [1 - far, far - 1, far] if far > 2 else [0, 1, -1, 2], "out")

    send_gate.wait_send()
    wait_bytes(sp.at[:, pl.ds(0, n - 1)], p_sem.at[0])
    for g in range(CHUNKS):
        if g > 0:
            sent_f(g)
        wait_bytes(so.at[g], o_sem.at[g, 0])
        for way in range(2):
            for k in range(far):
                for piece in range(PIECES):
                    ring(g, k, way, piece).wait_send()
    wait_bytes(mine_w, wy_sem.at[0])
    wait_bytes(far_w, wx_sem.at[0])


def per_device(gate_in, value_in, gate_out, filter_spectrum, skip, out_weight):
    n, nz, ns = lax.axis_size("ctx"), lax.axis_size("tensor"), lax.axis_size("section")
    toks, chans = gate_in.shape[1:]
    k1s, _, cols, _ = filter_spectrum.shape[1:]
    feats = out_weight.shape[2]
    rows = n * k1s
    each = chans // (n * CHUNKS)
    pairs = each // 2
    consts = tables(rows, cols, n)
    vmem = pl.BlockSpec(memory_space=pltpu.VMEM)
    anywhere = pl.BlockSpec(memory_space=pl.ANY)
    bf, f32 = jnp.bfloat16, jnp.float32
    dma = pltpu.SemaphoreType.DMA
    out = pl.pallas_call(
        functools.partial(kernel, n, nz, ns),
        out_shape=jax.ShapeDtypeStruct((toks, feats), bf),
        in_specs=[anywhere] * 4 + [pl.BlockSpec(memory_space=pltpu.SMEM)] + [anywhere] * (1 + len(consts)),
        out_specs=vmem,
        scratch_shapes=[
            pltpu.VMEM((k1s, 2, cols, chans), bf),
            pltpu.VMEM((2, 16 * cols, cols), f32),
            pltpu.VMEM((CHUNKS, n, pairs, 16, cols), bf),
            pltpu.VMEM((CHUNKS, n, each, 16, 2 * cols), bf),
            pltpu.VMEM((CHUNKS, pairs, 16 * n, cols), bf),
            pltpu.VMEM((CHUNKS, each, rows, 2 * cols), bf),
            pltpu.VMEM((CHUNKS, each, rows, 2 * cols), f32),
            pltpu.VMEM((CHUNKS, n, pairs, 16, cols), bf),
            pltpu.VMEM((CHUNKS, n, pairs, 16, cols), bf),
            pltpu.VMEM((CHUNKS, nz, toks // 2, cols), bf),
            pltpu.VMEM((n, *out_weight.shape[1:]), bf),
            pltpu.VMEM((toks, feats), f32),
            pltpu.VMEM((toks, chans), bf),
            pltpu.VMEM((toks, chans), bf),
            pltpu.VMEM((toks, chans), bf),
            *[pltpu.VMEM(c.shape, c.dtype) for c in (consts[-1], *consts[:-1])],
            dma((2 + CHUNKS,)),
            dma((2,)),
            dma((2,)),
            dma((CHUNKS, 2)),
            dma((CHUNKS, 2)),
            dma((2,)),
            dma((2,)),
            dma((CHUNKS, 2, nz // 2, PIECES)),
            dma((CHUNKS, 2, nz // 2, PIECES)),
            dma((2 + len(consts),)),
        ],
        cost_estimate=pl.CostEstimate(flops=6_000_000_000, bytes_accessed=8_000_000, transcendentals=0),
        compiler_params=pltpu.CompilerParams(
            collective_id=0, has_side_effects=True, vmem_limit_bytes=56 * 1024 * 1024
        ),
    )(gate_in[0], value_in[0], filter_spectrum[0], gate_out[0], skip.astype(f32), out_weight[0], *consts)
    return out[None]


def solution(mesh):
    placed = (
        P("section", "ctx", "tensor"),
        P("section", "ctx", "tensor"),
        P("section", "ctx", "tensor"),
        P("section", "ctx", None, None, "tensor"),
        P("section", "tensor"),
        P("section", "ctx", "tensor"),
    )
    return jax.shard_map(
        per_device,
        mesh=mesh,
        in_specs=placed,
        out_specs=P("section", "ctx", "tensor"),
        check_vma=False,
    )
```
